32 devices in a mesh: tile: 8 (over z, x), sec: 4 (over y, core).
Axes of the slice: x: 2, y: 2, z: 4, core: 2. Of those that a mesh axis runs over, the one named last changes fastest.
Arguments:
- displacement: float32 [8, 2, 128, 1024], P('sec', None, 'tile'), may hold values from -0.15 to 0.15
- velocity: float32 [8, 2, 128, 1024], P('sec', None, 'tile'), may hold values from -6 to 6
- stiffness: bfloat16 [8, 4, 128, 1024], P('sec', None, 'tile'), may hold values from 0.29882812 to 3
- anchor: float32 [2, 128, 1024], P(None, 'tile'), may hold values from -0.15 to 0.15
- match_source: int32 [8, 2048], P('sec', 'tile'), may hold values from 0 to 16383
- match_target: int32 [8, 2048], P('sec', 'tile'), may hold values from 0 to 16383
- match_weight: float32 [8, 2048], P('sec', 'tile'), may hold values from 1 to 8
- match_count: int32 [8, 8], P('sec', 'tile'), may hold values from 1 to 256, 1024 in all within a row
- reset_mask: int32 [2, 8], P(None, 'sec'), may hold values 0 or 1
Outputs:
- new_displacement: float32 [8, 2, 128, 1024], P('sec', None, 'tile')
- new_velocity: float32 [8, 2, 128, 1024], P('sec', None, 'tile')
The draws below stay inside these ranges and needn't reach their ends.
Inputs may be any that keep to these rules, and one draw needn't show every extreme that they name: `match_count`: in every section the largest count is 256.
All inputs are finite; a program needn't handle non-finite values. No bound on the sum of `match_count` or of `reset_mask` on one device may be relied on, other than what follows from the above.
Results may differ from the reference program's by a relative error of at most 0.00055.
Values may be sent and summed in bfloat16 or wider, within the bound.
A program may use at most 128 MiB of HBM per device.

```python
import math
import jax
import jax.numpy as jnp
import numpy as np
from jax import lax

ROWS_DEV = 16
COLS = 1024
MATCH_DEV = 256
ITERS = 2
SECTIONS = 8
ROWS = 128
SLOTS = 2048
N_TILE = 8


def draw_displacement(key, part):
    first_key = jax.random.fold_in(key, 0)
    ramp = (0.05 + 0.1 * jnp.arange(ROWS, dtype=jnp.float32) / ROWS)[:, None]
    shape = (SECTIONS, 2, ROWS, COLS)
    base = jax.random.uniform(first_key, shape, jnp.float32, -1.0, 1.0)
    return base * ramp


def draw_velocity(key, part):
    first_key = jax.random.fold_in(key, 0)
    ramp = (0.5 + jnp.arange(ROWS, dtype=jnp.float32) / ROWS)[:, None]
    shape = (SECTIONS, 2, ROWS, COLS)
    base = jax.random.truncated_normal(first_key, -3.0, 3.0, shape, jnp.float32)
    return base * ramp


def place_ends(entries, stream_key, smallest, top_value):
    longest = entries.shape.index(max(entries.shape))
    spots = []
    for shift in (0, 1):
        where = [jax.random.randint(jax.random.fold_in(stream_key, axis), (), 0, length) for axis, length in enumerate(entries.shape)]
        where[longest] = (where[longest] + shift) % entries.shape[longest]
        spots.append(tuple(where))
    return entries.at[spots[0]].set(smallest).at[spots[1]].set(top_value)


def block_levels(rng, shape, pieces, low, top_value):
    loudness = 1.0
    for dim, shards_of in pieces:
        heights = jax.random.uniform(jax.random.fold_in(jax.random.fold_in(rng, 6), dim), (shards_of,), jnp.float32, low / len(pieces), top_value / len(pieces))
        loudness = loudness * jnp.repeat(jnp.exp(heights), shape[dim] // shards_of).reshape((-1,) + (1,) * (len(shape) - 1 - dim))
    return loudness


def length_profile(count, total, most, slope):
    weights = [(1 << 20) // math.isqrt(rank ** slope) + 1 for rank in range(2, count + 1)]
    spare, holding = total - most - (count - 1), [1] * (count - 1)
    while spare > 0:
        candidates = [i for i in range(count - 1) if holding[i] < most]
        mass, remaining = sum([weights[i] for i in candidates]), spare
        for i in candidates:
            more = min(most - holding[i], max(1, remaining * weights[i] // mass), spare)
            holding[i] = holding[i] + more
            spare = spare - more
    return np.array([most] + holding)


def ragged_sizes(stream_key, count, total, bound, lean):
    if count == 2:
        one = jax.random.randint(stream_key, (), max(1, total - bound), min(bound, total - 1) + 1)
        return jnp.stack([one, total - one])
    sizes = jnp.asarray(length_profile(count, total, bound, lean), jnp.int32)
    pairs = (count - 1) // 2
    giver, taker = sizes[1:1 + 2 * pairs:2], sizes[2:2 + 2 * pairs:2]
    margin = jnp.minimum(giver - 1, bound - taker)
    shifted = jax.random.randint(jax.random.fold_in(stream_key, 1), (pairs,), 0, 1 << 20) % (margin + 1)
    sizes = sizes.at[1:1 + 2 * pairs:2].set(giver - shifted).at[2:2 + 2 * pairs:2].set(taker + shifted)
    return sizes[jax.random.permutation(jax.random.fold_in(stream_key, 2), count)]


def setup_inputs(seed: int = 0) -> dict:
    key_list = jax.random.split(jax.random.key(seed), 10)
    displacement = draw_displacement(jax.random.fold_in(key_list[9], 71), 0)
    velocity = draw_velocity(jax.random.fold_in(key_list[9], 71), 0)
    stiffness = jnp.clip(jnp.exp(math.log(3.0) - 2.306499 * jax.random.uniform(key_list[2], (SECTIONS, 4, ROWS, COLS), jnp.float32) ** block_levels(key_list[2], (SECTIONS, 4, ROWS, COLS), ((0, 4), (2, 8)), -0.2, 0.2)), 0.29882812, 3.0).astype(jnp.bfloat16)
    anchor = jnp.clip(jax.random.uniform(key_list[3], (2, ROWS, COLS), jnp.float32, -0.15, 0.15) * block_levels(key_list[3], (2, ROWS, COLS), ((1, 8),), -0.4, 0.0), -0.15, 0.15)
    match_source = place_ends(jax.random.randint(key_list[4], (SECTIONS, SLOTS), 0, ROWS_DEV * COLS), jax.random.fold_in(key_list[4], 1), 0, (ROWS_DEV * COLS) - 1).astype(jnp.int32)
    match_target = place_ends(jax.random.randint(key_list[5], (SECTIONS, SLOTS), 0, ROWS_DEV * COLS), jax.random.fold_in(key_list[5], 1), 0, (ROWS_DEV * COLS) - 1).astype(jnp.int32)
    match_weight = jnp.clip(jnp.exp(math.log(8.0) - 2.0794415 * jax.random.uniform(key_list[6], (SECTIONS, SLOTS), jnp.float32) ** block_levels(key_list[6], (SECTIONS, SLOTS), ((0, 4), (1, 8)), -0.2, 0.2)), 1.0, 8.0)
    match_count = jax.vmap(lambda own: ragged_sizes(own, N_TILE, N_TILE * MATCH_DEV // 2, MATCH_DEV, 2))(jax.random.split(key_list[7], SECTIONS)).reshape((SECTIONS, N_TILE)).astype(jnp.int32)
    reset_mask = place_ends((jax.random.randint(key_list[8], (ITERS, SECTIONS), 0, 4) < 1).astype(jnp.int32), jax.random.fold_in(key_list[8], 1), 0, 1)
    return {"displacement": displacement, "velocity": velocity, "stiffness": stiffness, "anchor": anchor, "match_source": match_source, "match_target": match_target, "match_weight": match_weight, "match_count": match_count, "reset_mask": reset_mask}


max_step = 0.05
time_step = 0.5
mixing = 0.1
epsilon = 1e-06
diagonal_rest = 1.4142135623730951

def from_left(values):
    return jnp.concatenate([jnp.zeros_like(values[..., :1]), values[..., :-1]], axis=-1)

def from_right(values):
    return jnp.concatenate([values[..., 1:], jnp.zeros_like(values[..., :1])], axis=-1)

def bond_force(first_gap, second_gap, spring_stiff, rest):
    stretch_len = jnp.sqrt(first_gap * first_gap + second_gap * second_gap)
    factor = spring_stiff * (stretch_len - rest) / stretch_len
    return (factor * first_gap, factor * second_gap)

def spring_force(padded, springs, row_start, total_rows):
    band_rows = padded.shape[-2] - 2
    columns = padded.shape[-1]
    stiff_all = springs.astype(jnp.float32)
    bond_rows = row_start - 1 + lax.iota(jnp.int32, band_rows + 1)
    row_valid = ((bond_rows >= 0) & (bond_rows + 1 < total_rows)).astype(jnp.float32)[:, None]
    column_ids = lax.iota(jnp.int32, columns)
    has_right = (column_ids < columns - 1).astype(jnp.float32)
    has_left = (column_ids >= 1).astype(jnp.float32)
    upper_first = padded[..., 0, :-1, :]
    upper_second = padded[..., 1, :-1, :]
    lower_first = padded[..., 0, 1:, :]
    lower_second = padded[..., 1, 1:, :]
    south = bond_force(1.0 + lower_first - upper_first, lower_second - upper_second, stiff_all[..., 1, :, :] * row_valid, 1.0)
    south_east = bond_force(1.0 + from_right(lower_first) - upper_first, 1.0 + from_right(lower_second) - upper_second, stiff_all[..., 2, :, :] * row_valid * has_right, diagonal_rest)
    south_west = bond_force(1.0 + from_left(lower_first) - upper_first, -1.0 + from_left(lower_second) - upper_second, stiff_all[..., 3, :, :] * row_valid * has_left, diagonal_rest)
    middle_first = padded[..., 0, 1:-1, :]
    middle_second = padded[..., 1, 1:-1, :]
    east = bond_force(from_right(middle_first) - middle_first, 1.0 + from_right(middle_second) - middle_second, stiff_all[..., 0, 1:, :] * has_right, 1.0)

    def summed(part):
        result = south[part][..., 1:, :] - south[part][..., :-1, :]
        result = result + south_east[part][..., 1:, :] - from_left(south_east[part][..., :-1, :])
        result = result + south_west[part][..., 1:, :] - from_right(south_west[part][..., :-1, :])
        return result + east[part] - from_left(east[part])
    return jnp.stack([summed(0), summed(1)], axis=-3)

def pick_nodes(values, index):
    return jax.vmap(lambda field, where: field[:, where])(values, index)

def place_nodes(target, index, amount):
    return jax.vmap(lambda field, where, extra: field.at[:, where].add(extra))(target, index, amount)

def reference(displacement, velocity, stiffness, anchor, match_source, match_target, match_weight, match_count, reset_mask):
    nodes = ROWS * COLS
    springs = jnp.concatenate([jnp.zeros((SECTIONS, 4, 1, COLS), jnp.bfloat16), stiffness], axis=2)
    slot_ids = lax.iota(jnp.int32, SLOTS)
    band_of = slot_ids // MATCH_DEV
    within = slot_ids % MATCH_DEV
    slot_live = (within[None, :] < match_count[:, band_of]).astype(jnp.float32)
    weight_live = match_weight * slot_live
    offset = (band_of * (ROWS_DEV * COLS)).astype(jnp.int32)
    source_node = match_source + offset[None, :]
    target_node = match_target + offset[None, :]
    current = displacement
    speed = velocity
    for iteration in range(ITERS):

        def section_force(pair):
            field, spring_part = pair
            padded = jnp.pad(field, ((0, 0), (1, 1), (0, 0)))
            return spring_force(padded, spring_part, 0, ROWS)
        force = lax.map(section_force, (current, springs)).reshape(SECTIONS, 2, nodes)
        flat = current.reshape(SECTIONS, 2, nodes)
        following = jnp.concatenate([flat[1:], anchor.reshape(1, 2, nodes)], axis=0)
        source_points = pick_nodes(flat, source_node)
        target_points = pick_nodes(following, target_node)
        match_force = weight_live[:, None, :] * (target_points - source_points)
        force = place_nodes(force, source_node, match_force)
        upper_part = place_nodes(force[1:], target_node[:-1], -match_force[:-1])
        force = jnp.concatenate([force[:1], upper_part], axis=0).reshape(SECTIONS, 2, ROWS, COLS)
        velocity_mid = speed + time_step * force
        force_sq = lax.optimization_barrier(jnp.sum(force * force, axis=(1, 2, 3)))
        speed_sq = lax.optimization_barrier(jnp.sum(velocity_mid * velocity_mid, axis=(1, 2, 3)))
        speed_ratio = jnp.sqrt(speed_sq) / jnp.sqrt(force_sq + epsilon)
        speed = (1.0 - mixing) * velocity_mid + mixing * speed_ratio[:, None, None, None] * force
        keep = (1 - reset_mask[iteration]).astype(jnp.float32)
        speed = speed * keep[:, None, None, None]
        current = current + max_step * jnp.tanh(time_step * speed / max_step)
    return (current, speed)
```

```python
import functools

import jax
import jax.numpy as jnp
from jax import lax
from jax.experimental import pallas as pl
from jax.experimental.pallas import tpu as pltpu
from jax.sharding import PartitionSpec as P

ITERS = 2

max_step = 0.05
time_step = 0.5
mixing = 0.1
epsilon = 1e-06
diagonal_rest = 1.4142135623730951
MESH = pl.DeviceIdType.MESH
F32 = jnp.float32
BF16 = jnp.bfloat16


def split(value):
    high = value.astype(BF16)
    return high, (value - high.astype(F32)).astype(BF16)


def from_left(values):
    return pltpu.roll(values, 1, 1)


def from_right(values):
    return pltpu.roll(values, values.shape[1] - 1, 1)


def bond(first_gap, second_gap, stiff, rest):
    inverse = lax.rsqrt(first_gap * first_gap + second_gap * second_gap)
    factor = stiff * (1.0 - rest * inverse)
    return factor * first_gap, factor * second_gap


def downward(upper, lower, lower_right, lower_left, stiff):
    south = bond(1.0 + lower[0] - upper[0], lower[1] - upper[1], stiff[0], 1.0)
    east = bond(
        1.0 + lower_right[0] - upper[0], 1.0 + lower_right[1] - upper[1], stiff[1], diagonal_rest
    )
    west = bond(
        1.0 + lower_left[0] - upper[0], lower_left[1] - upper[1] - 1.0, stiff[2], diagonal_rest
    )
    owned = tuple(south[i] + east[i] + west[i] for i in range(2))
    ended = tuple(south[i] + from_left(east[i]) + from_right(west[i]) for i in range(2))
    return owned, ended


def stacked(grid, rows):
    columns = grid.shape[1]
    return jnp.concatenate([grid[:, i : i + 128] for i in range(0, columns, 128)], axis=0)


def unstacked(values, rows):
    return jnp.concatenate([values[i : i + rows] for i in range(0, values.shape[0], rows)], axis=1)


def tables(index, rows, columns):
    pieces = columns // 128
    slots = index.shape[1]
    low = lax.rem(index, 128)
    row = index // columns
    place = (lax.rem(index, columns) // 128) * rows + row
    column_table = (lax.broadcasted_iota(jnp.int32, (128, slots), 0) == low).astype(F32).astype(BF16)
    row_table = (lax.broadcasted_iota(jnp.int32, (pieces * rows, slots), 0) == place).astype(F32)
    return column_table, row_table


def pick(parts, column_table, row_table):
    result = []
    for high, low in parts:
        found = jnp.dot(high, column_table, preferred_element_type=F32)
        found = found + jnp.dot(low, column_table, preferred_element_type=F32)
        result.append(jnp.sum(found * row_table, axis=0, keepdims=True))
    return result


def place(amount, column_table, row_table, rows):
    spread = amount * row_table
    high, low = split(spread)
    dims = (((1,), (1,)), ((), ()))
    out = lax.dot_general(high, column_table, dims, preferred_element_type=F32)
    out = out + lax.dot_general(low, column_table, dims, preferred_element_type=F32)
    return unstacked(out, rows)


def kernel(
    n_tile,
    n_sec,
    u_hbm,
    v_hbm,
    k_hbm,
    a_hbm,
    src_hbm,
    tgt_hbm,
    w_hbm,
    cnt,
    rst,
    out_u,
    out_v,
    u_ref,
    v_ref,
    k_ref,
    a_ref,
    src_ref,
    tgt_ref,
    w_ref,
    kf_ref,
    force_ref,
    mid_ref,
    ctab_ref,
    rtab_ref,
    in_sem,
    out_sem,
    down_send,
    up_send,
    down_recv,
    up_recv,
    edge_send,
    edge_recv,
    slot_send,
    slot_recv,
    points_send,
    points_recv,
    sums_send,
    sums_recv,
    near_ssem,
    near_rsem,
    sums_ssem,
    sums_rsem,
):
    tile = lax.axis_index("tile")
    sec = lax.axis_index("sec")
    sections, _, rows, columns = u_ref.shape
    slots = src_ref.shape[1]
    below, above = lax.rem(tile + 1, n_tile), lax.rem(tile + n_tile - 1, n_tile)
    after, before = lax.rem(sec + 1, n_sec), lax.rem(sec + n_sec - 1, n_sec)

    loads = [
        pltpu.make_async_copy(source, target, in_sem.at[i])
        for i, (source, target) in enumerate(
            [
                (u_hbm, u_ref),
                (k_hbm, k_ref),
                (src_hbm, src_ref),
                (tgt_hbm, tgt_ref),
                (w_hbm, w_ref),
                (a_hbm, a_ref),
                (v_hbm, v_ref),
            ]
        )
    ]
    for load in loads:
        load.start()

    barrier = pltpu.get_barrier_semaphore()
    for step in range(1, n_tile):
        pl.semaphore_signal(
            barrier, inc=1, device_id=(lax.rem(tile + step, n_tile), sec), device_id_type=MESH
        )
    for other in (after, before):
        pl.semaphore_signal(barrier, inc=1, device_id=(tile, other), device_id_type=MESH)

    def remote(source, target, ssem, rsem, device):
        copy = pltpu.make_async_remote_copy(
            src_ref=source,
            dst_ref=target,
            send_sem=ssem,
            recv_sem=rsem,
            device_id=device,
            device_id_type=MESH,
        )
        copy.start()
        return copy

    def near(number, source, target, device):
        return remote(source, target, near_ssem.at[number], near_rsem.at[number], device)

    for load in loads[:5]:
        load.wait()

    column_ids = lax.broadcasted_iota(jnp.int32, (1, columns), 1)
    has_right = (column_ids < columns - 1).astype(F32)
    has_left = (column_ids >= 1).astype(F32)
    for s in range(sections):
        for i in range(2):
            down_send[2 * s + i : 2 * s + i + 1, :] = u_ref[s, i, rows - 1 : rows, :]
            up_send[2 * s + i : 2 * s + i + 1, :] = u_ref[s, i, 0:1, :]
        for kind in range(4):
            stiff = k_ref[s, kind].astype(F32)
            if kind in (0, 2):
                stiff = stiff * has_right
            if kind == 3:
                stiff = stiff * has_left
            kf_ref[s, kind] = stiff
            if kind > 0:
                at = 8 + 2 * (kind - 1) + s
                down_send[at : at + 1, :] = stiff[rows - 1 : rows, :]

    slot_ids = lax.broadcasted_iota(jnp.int32, (1, slots), 1)
    weights = [
        w_ref[s : s + 1, :] * (slot_ids < cnt[s, 0]).astype(F32) for s in range(sections)
    ]

    def store_tables(number, index):
        column_table, row_table = tables(index, rows, columns)
        ctab_ref[number] = column_table
        rtab_ref[number] = row_table

    def picked(number, parts):
        return pick(parts, ctab_ref[number], rtab_ref[number])

    def placed(number, amount):
        return place(amount, ctab_ref[number], rtab_ref[number], rows)

    def parts_of(ref, s=None):
        return [
            split(stacked(ref[i] if s is None else ref[s, i], rows)) for i in range(2)
        ]

    store_tables(1, src_ref[1:2, :])
    parts_1 = parts_of(u_ref, 1)
    points_1 = picked(1, parts_1)
    slot_send[0, 0:1, :] = tgt_ref[1:2, :].astype(F32)
    slot_send[0, 1:2, :] = weights[1]
    slot_send[0, 2:3, :] = points_1[0]
    slot_send[0, 3:4, :] = points_1[1]

    pl.semaphore_wait(barrier, n_tile + 1)
    copies = [
        near(0, slot_send.at[0], slot_recv.at[0], (tile, after)),
        near(1, down_send, down_recv, (below, sec)),
        near(2, up_send, up_recv, (above, sec)),
    ]
    slots_in, down_in, up_in = copies

    store_tables(0, src_ref[0:1, :])
    store_tables(2, tgt_ref[0:1, :])
    parts_0 = parts_of(u_ref, 0)
    points_0 = picked(0, parts_0)
    ends_0 = picked(2, parts_1)
    loads[5].wait()
    first_sec = sec == 0

    def slab_parts():
        return [
            split(stacked(jnp.where(first_sec, a_ref[i], u_ref[0, i]), rows)) for i in range(2)
        ]

    slots_in.wait_recv()
    store_tables(3, slot_recv[0, 0:1, :].astype(jnp.int32))
    weight_in = slot_recv[0, 1:2, :] * jnp.where(first_sec, 0.0, 1.0)
    ends_in = picked(3, slab_parts())
    points_in = [slot_recv[0, 2:3, :], slot_recv[0, 3:4, :]]
    points_send[0, 0:1, :] = ends_in[0]
    points_send[0, 1:2, :] = ends_in[1]
    points = near(3, points_send.at[0], points_recv.at[0], (tile, before))
    copies.append(points)

    loads[6].wait()
    not_last = jnp.where(tile == n_tile - 1, 0.0, 1.0)
    not_first = jnp.where(tile == 0, 0.0, 1.0)
    row_ids = lax.broadcasted_iota(jnp.int32, (rows, columns), 0)
    row_valid = jnp.where(row_ids == rows - 1, not_last, 1.0)
    for s in range(sections):
        for kind in range(1, 4):
            kf_ref[s, kind] = kf_ref[s, kind] * row_valid

    down_in.wait_recv()
    up_in.wait_recv()
    halo_up = down_recv[0:4, :]
    halo_down = up_recv[0:4, :]
    stiff_up = [down_recv[8 + 2 * i : 10 + 2 * i, :] * not_first for i in range(3)]
    speed_ratio = None

    for iteration in range(ITERS):
        upper = [
            jnp.concatenate([halo_up[i : i + 1], halo_up[2 + i : 3 + i]], axis=0)
            for i in range(2)
        ]
        lower = [
            jnp.concatenate([u_ref[0, i, 0:1, :], u_ref[1, i, 0:1, :]], axis=0)
            for i in range(2)
        ]
        _, ended_up = downward(
            upper,
            lower,
            [from_right(x) for x in lower],
            [from_left(x) for x in lower],
            stiff_up,
        )
        for s in range(sections):
            own = [u_ref[s, i] for i in range(2)]
            right = [from_right(x) for x in own]
            left = [from_left(x) for x in own]
            tail = [halo_down[2 * s + i : 2 * s + i + 1] for i in range(2)]
            lower = [jnp.concatenate([own[i][1:], tail[i]], axis=0) for i in range(2)]
            lower_right = [
                jnp.concatenate([right[i][1:], from_right(tail[i])], axis=0) for i in range(2)
            ]
            lower_left = [
                jnp.concatenate([left[i][1:], from_left(tail[i])], axis=0) for i in range(2)
            ]
            owned, ended = downward(
                own, lower, lower_right, lower_left, [kf_ref[s, kind] for kind in (1, 2, 3)]
            )
            east = bond(right[0] - own[0], 1.0 + right[1] - own[1], kf_ref[s, 0], 1.0)
            for i in range(2):
                incoming = jnp.concatenate(
                    [ended_up[i][s : s + 1], ended[i][: rows - 1]], axis=0
                )
                force_ref[s, i] = owned[i] + east[i] - from_left(east[i]) - incoming

        match_0 = [weights[0] * (ends_0[i] - points_0[i]) for i in range(2)]
        match_in = [weight_in * (ends_in[i] - points_in[i]) for i in range(2)]
        points.wait_recv()
        sums = []
        for i in range(2):
            found = points_recv[iteration, i : i + 1, :]
            match_1 = weights[1] * (found - points_1[i])
            force_ref[0, i] = force_ref[0, i] + placed(0, match_0[i]) - placed(3, match_in[i])
            force_ref[1, i] = force_ref[1, i] + placed(1, match_1) - placed(2, match_0[i])

        for s in range(sections):
            force_sq, speed_sq = 0.0, 0.0
            for i in range(2):
                force = force_ref[s, i]
                middle = v_ref[s, i] + time_step * force
                mid_ref[s, i] = middle
                force_sq = force_sq + jnp.sum(force * force, axis=0, keepdims=True)
                speed_sq = speed_sq + jnp.sum(middle * middle, axis=0, keepdims=True)
                if iteration < ITERS - 1:
                    at = 2 * s + i
                    edge_send[0, at : at + 1, :] = force[rows - 1 : rows, :]
                    edge_send[0, 4 + at : 5 + at, :] = middle[rows - 1 : rows, :]
                    edge_send[1, at : at + 1, :] = force[0:1, :]
                    edge_send[1, 4 + at : 5 + at, :] = middle[0:1, :]
            for at, value in ((s, force_sq), (2 + s, speed_sq)):
                narrow = value[:, 0:128]
                for piece in range(128, columns, 128):
                    narrow = narrow + value[:, piece : piece + 128]
                sums_send[iteration, at : at + 1, :] = narrow
        peers = []
        for step in range(n_tile - 1, 0, -1):
            peers.append(
                remote(
                    sums_send.at[iteration],
                    sums_recv.at[iteration, step - 1],
                    sums_ssem.at[iteration, step - 1],
                    sums_rsem.at[iteration, step - 1],
                    (lax.rem(tile + step, n_tile), sec),
                )
            )
        copies += peers
        if iteration < ITERS - 1:
            edge_down = near(4, edge_send.at[0], edge_recv.at[0], (below, sec))
            edge_up = near(5, edge_send.at[1], edge_recv.at[1], (above, sec))
            copies += [edge_down, edge_up]

        total = sums_send[iteration, 0:4, :]
        for peer in peers:
            peer.wait_recv()
        for step in range(n_tile - 1):
            total = total + sums_recv[iteration, step, 0:4, :]
        total = jnp.sum(total, axis=1, keepdims=True)
        ratio = jnp.sqrt(total[2:4]) / jnp.sqrt(total[0:2] + epsilon)
        keep = [(1 - rst[iteration, s]).astype(F32) for s in range(sections)]

        for s in range(sections):
            push = mixing * ratio[s : s + 1, :]
            for i in range(2):
                speed = ((1.0 - mixing) * mid_ref[s, i] + push * force_ref[s, i]) * keep[s]
                v_ref[s, i] = speed
                u_ref[s, i] = u_ref[s, i] + max_step * jnp.tanh(time_step / max_step * speed)

        if iteration < ITERS - 1:
            parts_1 = parts_of(u_ref, 1)
            points_1 = picked(1, parts_1)
            slot_send[1, 0:1, :] = points_1[0]
            slot_send[1, 1:2, :] = points_1[1]
            slots_in = near(6, slot_send.at[1], slot_recv.at[1], (tile, after))
            ends_in = picked(3, slab_parts())
            points_send[1, 0:1, :] = ends_in[0]
            points_send[1, 1:2, :] = ends_in[1]
            points = near(7, points_send.at[1], points_recv.at[1], (tile, before))
            copies += [slots_in, points]
            points_0 = picked(0, parts_of(u_ref, 0))
            ends_0 = picked(2, parts_1)

            half = lax.broadcasted_iota(jnp.int32, (4, columns), 0) < 2
            ratio_rows = jnp.where(half, mixing * ratio[0:1, :], mixing * ratio[1:2, :])
            keep_rows = jnp.where(half, keep[0], keep[1])

            def moved(halo, edge):
                speed = ((1.0 - mixing) * edge[4:8, :] + ratio_rows * edge[0:4, :]) * keep_rows
                return halo + max_step * jnp.tanh(time_step / max_step * speed)

            edge_down.wait_recv()
            edge_up.wait_recv()
            halo_up = moved(halo_up, edge_recv[0])
            halo_down = moved(halo_down, edge_recv[1])
            slots_in.wait_recv()
            points_in = [slot_recv[1, 0:1, :], slot_recv[1, 1:2, :]]

    stores = [
        pltpu.make_async_copy(v_ref, out_v, out_sem.at[0]),
        pltpu.make_async_copy(u_ref, out_u, out_sem.at[1]),
    ]
    for store in stores:
        store.start()
    for copy in copies:
        copy.wait_send()
    for store in stores:
        store.wait()


def local(n_tile, n_sec, *arguments):
    displacement, velocity, stiffness, anchor, source, target, weight, _, _ = arguments
    sections, _, rows, columns = displacement.shape
    slots = source.shape[1]
    pieces = columns // 128
    dma = pltpu.SemaphoreType.DMA
    anywhere = pl.BlockSpec(memory_space=pl.ANY)
    scalars = pl.BlockSpec(memory_space=pltpu.SMEM)
    field = jax.ShapeDtypeStruct(displacement.shape, F32)
    vmem = pltpu.VMEM
    return pl.pallas_call(
        functools.partial(kernel, n_tile, n_sec),
        out_shape=(field, field),
        in_specs=[anywhere] * 7 + [scalars] * 2,
        out_specs=(anywhere, anywhere),
        scratch_shapes=[
            vmem(displacement.shape, F32),
            vmem(velocity.shape, F32),
            vmem(stiffness.shape, BF16),
            vmem(anchor.shape, F32),
            vmem(source.shape, jnp.int32),
            vmem(target.shape, jnp.int32),
            vmem(weight.shape, F32),
            vmem(stiffness.shape, F32),
            vmem(displacement.shape, F32),
            vmem(displacement.shape, F32),
            vmem((4, 128, slots), BF16),
            vmem((4, pieces * rows, slots), F32),
            dma((7,)),
            dma((2,)),
            vmem((16, columns), F32),
            vmem((8, columns), F32),
            vmem((16, columns), F32),
            vmem((8, columns), F32),
            vmem((2, 8, columns), F32),
            vmem((2, 8, columns), F32),
            vmem((2, 8, slots), F32),
            vmem((2, 8, slots), F32),
            vmem((2, 8, slots), F32),
            vmem((2, 8, slots), F32),
            vmem((ITERS, 8, 128), F32),
            vmem((ITERS, n_tile - 1, 8, 128), F32),
            dma((8,)),
            dma((8,)),
            dma((ITERS, n_tile - 1)),
            dma((ITERS, n_tile - 1)),
        ],
        compiler_params=pltpu.CompilerParams(
            collective_id=0, has_side_effects=True, vmem_limit_bytes=60 * 1024 * 1024
        ),
        cost_estimate=pl.CostEstimate(
            flops=40_000_000, bytes_accessed=1_500_000, transcendentals=1_000_000
        ),
    )(*arguments)


def solution(mesh):
    placed = (
        P("sec", None, "tile", None),
        P("sec", None, "tile", None),
        P("sec", None, "tile", None),
        P(None, "tile", None),
        P("sec", "tile"),
        P("sec", "tile"),
        P("sec", "tile"),
        P("sec", "tile"),
        P(None, "sec"),
    )
    return jax.shard_map(
        functools.partial(local, mesh.shape["tile"], mesh.shape["sec"]),
        mesh=mesh,
        in_specs=placed,
        out_specs=(P("sec", None, "tile", None), P("sec", None, "tile", None)),
        check_vma=False,
    )
```

```python
import functools

import jax
import jax.numpy as jnp
from jax import lax
from jax.experimental import pallas as pl
from jax.experimental.pallas import tpu as pltpu
from jax.sharding import PartitionSpec as P

ITERS = 2

max_step = 0.05
time_step = 0.5
mixing = 0.1
epsilon = 1e-06
diagonal_rest = 1.4142135623730951
MESH = pl.DeviceIdType.MESH
F32 = jnp.float32
BF16 = jnp.bfloat16


def split(value):
    high = value.astype(BF16)
    return high, (value - high.astype(F32)).astype(BF16)


def from_left(values):
    return pltpu.roll(values, 1, 1)


def from_right(values):
    return pltpu.roll(values, values.shape[1] - 1, 1)


def bond(first_gap, second_gap, stiff, rest):
    inverse = lax.rsqrt(first_gap * first_gap + second_gap * second_gap)
    factor = stiff * (1.0 - rest * inverse)
    return factor * first_gap, factor * second_gap


def downward(upper, lower, lower_right, lower_left, stiff):
    south = bond(1.0 + lower[0] - upper[0], lower[1] - upper[1], stiff[0], 1.0)
    east = bond(
        1.0 + lower_right[0] - upper[0], 1.0 + lower_right[1] - upper[1], stiff[1], diagonal_rest
    )
    west = bond(
        1.0 + lower_left[0] - upper[0], lower_left[1] - upper[1] - 1.0, stiff[2], diagonal_rest
    )
    owned = tuple(south[i] + east[i] + west[i] for i in range(2))
    ended = tuple(south[i] + from_left(east[i]) + from_right(west[i]) for i in range(2))
    return owned, ended


def stacked(grid, rows):
    columns = grid.shape[1]
    return jnp.concatenate([grid[:, i : i + 128] for i in range(0, columns, 128)], axis=0)


def unstacked(values, rows):
    return jnp.concatenate([values[i : i + rows] for i in range(0, values.shape[0], rows)], axis=1)


def tables(index, rows, columns):
    pieces = columns // 128
    slots = index.shape[1]
    low = lax.rem(index, 128)
    row = index // columns
    place = (lax.rem(index, columns) // 128) * rows + row
    column_table = (lax.broadcasted_iota(jnp.int32, (128, slots), 0) == low).astype(F32).astype(BF16)
    row_table = (lax.broadcasted_iota(jnp.int32, (pieces * rows, slots), 0) == place).astype(F32)
    return column_table, row_table


def pick(parts, column_table, row_table):
    found = jnp.dot(parts, column_table, preferred_element_type=F32)
    nodes = row_table.shape[0]
    result = []
    for i in range(2):
        both = found[i * nodes : (i + 1) * nodes] + found[(2 + i) * nodes : (3 + i) * nodes]
        result.append(jnp.sum(both * row_table, axis=0, keepdims=True))
    return result


def place(amounts, column_table, row_table, rows):
    highs = [amount.astype(BF16).astype(F32) for amount in amounts]
    lows = [amount - high for amount, high in zip(amounts, highs)]
    spread = jnp.concatenate([(x * row_table).astype(BF16) for x in highs + lows], axis=0)
    out = lax.dot_general(
        spread, column_table, (((1,), (1,)), ((), ())), preferred_element_type=F32
    )
    nodes = row_table.shape[0]
    return [
        unstacked(out[i * nodes : (i + 1) * nodes] + out[(2 + i) * nodes : (3 + i) * nodes], rows)
        for i in range(2)
    ]


def kernel(
    n_tile,
    n_sec,
    u_hbm,
    v_hbm,
    k_hbm,
    a_hbm,
    src_hbm,
    tgt_hbm,
    w_hbm,
    cnt,
    rst,
    out_mid,
    out_force,
    out_u,
    out_push,
    out_decay,
    u_ref,
    v_ref,
    k_ref,
    a_ref,
    src_ref,
    tgt_ref,
    w_ref,
    kf_ref,
    force_ref,
    mid_ref,
    ctab_ref,
    rtab_ref,
    push_ref,
    decay_ref,
    in_sem,
    out_sem,
    down_send,
    up_send,
    down_recv,
    up_recv,
    edge_send,
    edge_recv,
    slot_send,
    slot_recv,
    points_send,
    points_recv,
    sums_send,
    sums_recv,
    near_ssem,
    near_rsem,
    sums_ssem,
    sums_rsem,
):
    tile = lax.axis_index("tile")
    sec = lax.axis_index("sec")
    sections, _, rows, columns = u_ref.shape
    slots = src_ref.shape[1]
    below, above = lax.rem(tile + 1, n_tile), lax.rem(tile + n_tile - 1, n_tile)
    after, before = lax.rem(sec + 1, n_sec), lax.rem(sec + n_sec - 1, n_sec)

    loads = [
        pltpu.make_async_copy(source, target, in_sem.at[i])
        for i, (source, target) in enumerate(
            [
                (u_hbm, u_ref),
                (k_hbm, k_ref),
                (src_hbm, src_ref),
                (tgt_hbm, tgt_ref),
                (w_hbm, w_ref),
                (a_hbm, a_ref),
                (v_hbm, v_ref),
            ]
        )
    ]
    for load in loads:
        load.start()

    barrier = pltpu.get_barrier_semaphore()
    for step in range(1, n_tile):
        pl.semaphore_signal(
            barrier, inc=1, device_id=(lax.rem(tile + step, n_tile), sec), device_id_type=MESH
        )
    for other in (after, before):
        pl.semaphore_signal(barrier, inc=1, device_id=(tile, other), device_id_type=MESH)

    def remote(source, target, ssem, rsem, device):
        copy = pltpu.make_async_remote_copy(
            src_ref=source,
            dst_ref=target,
            send_sem=ssem,
            recv_sem=rsem,
            device_id=device,
            device_id_type=MESH,
        )
        copy.start()
        return copy

    def near(number, source, target, device):
        return remote(source, target, near_ssem.at[number], near_rsem.at[number], device)

    for load in loads[:5]:
        load.wait()

    column_ids = lax.broadcasted_iota(jnp.int32, (1, columns), 1)
    has_right = (column_ids < columns - 1).astype(F32)
    has_left = (column_ids >= 1).astype(F32)
    for s in range(sections):
        for i in range(2):
            down_send[2 * s + i : 2 * s + i + 1, :] = u_ref[s, i, rows - 1 : rows, :]
            up_send[2 * s + i : 2 * s + i + 1, :] = u_ref[s, i, 0:1, :]
        for kind in range(4):
            stiff = k_ref[s, kind].astype(F32)
            if kind in (0, 2):
                stiff = stiff * has_right
            if kind == 3:
                stiff = stiff * has_left
            kf_ref[s, kind] = stiff
            if kind > 0:
                at = 8 + 2 * (kind - 1) + s
                down_send[at : at + 1, :] = stiff[rows - 1 : rows, :]

    slot_ids = lax.broadcasted_iota(jnp.int32, (1, slots), 1)
    weights = [
        w_ref[s : s + 1, :] * (slot_ids < cnt[0, s]).astype(F32) for s in range(sections)
    ]

    def store_tables(section, half, index):
        column_table, row_table = tables(index, rows, columns)
        ctab_ref[section, :, half * slots : (half + 1) * slots] = column_table
        rtab_ref[section, :, half * slots : (half + 1) * slots] = row_table

    def picked(section, half, parts):
        lanes = slice(half * slots, (half + 1) * slots)
        return pick(parts, ctab_ref[section, :, lanes], rtab_ref[section, :, lanes])

    def picked_both(section, parts):
        both = pick(parts, ctab_ref[section], rtab_ref[section])
        return [x[:, :slots] for x in both], [x[:, slots:] for x in both]

    def split_parts(grids):
        pairs = [split(stacked(grid, rows)) for grid in grids]
        return jnp.concatenate([pairs[0][0], pairs[1][0], pairs[0][1], pairs[1][1]], axis=0)

    def parts_of(section):
        return split_parts([u_ref[section, i] for i in range(2)])

    store_tables(1, 0, src_ref[1:2, :])
    store_tables(1, 1, tgt_ref[0:1, :])
    points_1, ends_0 = picked_both(1, parts_of(1))
    slot_send[0, 0:1, :] = tgt_ref[1:2, :].astype(F32)
    slot_send[0, 1:2, :] = weights[1]
    slot_send[0, 2:3, :] = points_1[0]
    slot_send[0, 3:4, :] = points_1[1]

    pl.semaphore_wait(barrier, n_tile + 1)
    copies = [
        near(0, slot_send.at[0], slot_recv.at[0], (tile, after)),
        near(1, down_send, down_recv, (below, sec)),
        near(2, up_send, up_recv, (above, sec)),
    ]
    slots_in, down_in, up_in = copies

    store_tables(0, 0, src_ref[0:1, :])
    points_0 = picked(0, 0, parts_of(0))
    loads[5].wait()
    first_sec = sec == 0

    def slab_parts():
        return split_parts([jnp.where(first_sec, a_ref[i], u_ref[0, i]) for i in range(2)])

    slots_in.wait_recv()
    store_tables(0, 1, slot_recv[0, 0:1, :].astype(jnp.int32))
    weight_in = slot_recv[0, 1:2, :] * jnp.where(first_sec, 0.0, 1.0)
    ends_in = picked(0, 1, slab_parts())
    points_in = [slot_recv[0, 2:3, :], slot_recv[0, 3:4, :]]
    points_send[0, 0:1, :] = ends_in[0]
    points_send[0, 1:2, :] = ends_in[1]
    points = near(3, points_send.at[0], points_recv.at[0], (tile, before))
    copies.append(points)

    loads[6].wait()
    not_last = jnp.where(tile == n_tile - 1, 0.0, 1.0)
    not_first = jnp.where(tile == 0, 0.0, 1.0)
    row_ids = lax.broadcasted_iota(jnp.int32, (rows, columns), 0)
    row_valid = jnp.where(row_ids == rows - 1, not_last, 1.0)
    for s in range(sections):
        for kind in range(1, 4):
            kf_ref[s, kind] = kf_ref[s, kind] * row_valid

    down_in.wait_recv()
    up_in.wait_recv()
    halo_up = down_recv[0:4, :]
    halo_down = up_recv[0:4, :]
    stiff_up = [down_recv[8 + 2 * i : 10 + 2 * i, :] * not_first for i in range(3)]
    speed_ratio = None

    for iteration in range(ITERS):
        upper = [
            jnp.concatenate([halo_up[i : i + 1], halo_up[2 + i : 3 + i]], axis=0)
            for i in range(2)
        ]
        lower = [
            jnp.concatenate([u_ref[0, i, 0:1, :], u_ref[1, i, 0:1, :]], axis=0)
            for i in range(2)
        ]
        _, ended_up = downward(
            upper,
            lower,
            [from_right(x) for x in lower],
            [from_left(x) for x in lower],
            stiff_up,
        )
        for s in range(sections):
            own = [u_ref[s, i] for i in range(2)]
            right = [from_right(x) for x in own]
            left = [from_left(x) for x in own]
            tail = [halo_down[2 * s + i : 2 * s + i + 1] for i in range(2)]
            lower = [jnp.concatenate([own[i][1:], tail[i]], axis=0) for i in range(2)]
            lower_right = [
                jnp.concatenate([right[i][1:], from_right(tail[i])], axis=0) for i in range(2)
            ]
            lower_left = [
                jnp.concatenate([left[i][1:], from_left(tail[i])], axis=0) for i in range(2)
            ]
            owned, ended = downward(
                own, lower, lower_right, lower_left, [kf_ref[s, kind] for kind in (1, 2, 3)]
            )
            east = bond(right[0] - own[0], 1.0 + right[1] - own[1], kf_ref[s, 0], 1.0)
            for i in range(2):
                incoming = jnp.concatenate(
                    [ended_up[i][s : s + 1], ended[i][: rows - 1]], axis=0
                )
                force_ref[s, i] = owned[i] + east[i] - from_left(east[i]) - incoming

        match_0 = [weights[0] * (ends_0[i] - points_0[i]) for i in range(2)]
        match_in = [weight_in * (ends_in[i] - points_in[i]) for i in range(2)]
        added = place(
            [jnp.concatenate([match_0[i], -match_in[i]], axis=1) for i in range(2)],
            ctab_ref[0],
            rtab_ref[0],
            rows,
        )
        for i in range(2):
            force_ref[0, i] = force_ref[0, i] + added[i]
        points.wait_recv()
        match_1 = [
            weights[1] * (points_recv[iteration, i : i + 1, :] - points_1[i]) for i in range(2)
        ]
        added = place(
            [jnp.concatenate([match_1[i], -match_0[i]], axis=1) for i in range(2)],
            ctab_ref[1],
            rtab_ref[1],
            rows,
        )
        for i in range(2):
            force_ref[1, i] = force_ref[1, i] + added[i]

        for s in range(sections):
            force_sq, speed_sq = 0.0, 0.0
            for i in range(2):
                force = force_ref[s, i]
                middle = v_ref[s, i] + time_step * force
                mid_ref[s, i] = middle
                force_sq = force_sq + jnp.sum(force * force, axis=0, keepdims=True)
                speed_sq = speed_sq + jnp.sum(middle * middle, axis=0, keepdims=True)
                if iteration < ITERS - 1:
                    at = 2 * s + i
                    edge_send[0, at : at + 1, :] = force[rows - 1 : rows, :]
                    edge_send[0, 4 + at : 5 + at, :] = middle[rows - 1 : rows, :]
                    edge_send[1, at : at + 1, :] = force[0:1, :]
                    edge_send[1, 4 + at : 5 + at, :] = middle[0:1, :]
            for at, value in ((s, force_sq), (2 + s, speed_sq)):
                narrow = value[:, 0:128]
                for piece in range(128, columns, 128):
                    narrow = narrow + value[:, piece : piece + 128]
                sums_send[iteration, at : at + 1, :] = narrow
        peers = []
        for step in range(n_tile - 1, 0, -1):
            peers.append(
                remote(
                    sums_send.at[iteration],
                    sums_recv.at[iteration, step - 1],
                    sums_ssem.at[iteration, step - 1],
                    sums_rsem.at[iteration, step - 1],
                    (lax.rem(tile + step, n_tile), sec),
                )
            )
        copies += peers
        if iteration < ITERS - 1:
            edge_down = near(4, edge_send.at[0], edge_recv.at[0], (below, sec))
            edge_up = near(5, edge_send.at[1], edge_recv.at[1], (above, sec))
            copies += [edge_down, edge_up]

        if iteration == ITERS - 1:
            stores = [
                pltpu.make_async_copy(source, target, out_sem.at[i])
                for i, (source, target) in enumerate(
                    [(mid_ref, out_mid), (force_ref, out_force), (u_ref, out_u)]
                )
            ]
            for store in stores:
                store.start()

        total = sums_send[iteration, 0:4, :]
        for peer in peers:
            peer.wait_recv()
        for step in range(n_tile - 1):
            total = total + sums_recv[iteration, step, 0:4, :]
        total = jnp.sum(total, axis=1, keepdims=True)
        ratio = jnp.sqrt(total[2:4]) / jnp.sqrt(total[0:2] + epsilon)
        keep = [(1 - rst[iteration, s]).astype(F32) for s in range(sections)]

        if iteration == ITERS - 1:
            for s in range(sections):
                push_ref[s : s + 1, :] = jnp.broadcast_to(
                    mixing * ratio[s : s + 1, :] * keep[s], (1, columns)
                )
                decay_ref[s : s + 1, :] = jnp.full((1, columns), (1.0 - mixing) * keep[s], F32)
            break

        for s in range(sections):
            push = mixing * ratio[s : s + 1, :]
            for i in range(2):
                speed = ((1.0 - mixing) * mid_ref[s, i] + push * force_ref[s, i]) * keep[s]
                v_ref[s, i] = speed
                u_ref[s, i] = u_ref[s, i] + max_step * jnp.tanh(time_step / max_step * speed)

        if iteration < ITERS - 1:
            points_1, ends_0 = picked_both(1, parts_of(1))
            slot_send[1, 0:1, :] = points_1[0]
            slot_send[1, 1:2, :] = points_1[1]
            slots_in = near(6, slot_send.at[1], slot_recv.at[1], (tile, after))
            ends_in = picked(0, 1, slab_parts())
            points_send[1, 0:1, :] = ends_in[0]
            points_send[1, 1:2, :] = ends_in[1]
            points = near(7, points_send.at[1], points_recv.at[1], (tile, before))
            copies += [slots_in, points]
            points_0 = picked(0, 0, parts_of(0))

            half = lax.broadcasted_iota(jnp.int32, (4, columns), 0) < 2
            ratio_rows = jnp.where(half, mixing * ratio[0:1, :], mixing * ratio[1:2, :])
            keep_rows = jnp.where(half, keep[0], keep[1])

            def moved(halo, edge):
                speed = ((1.0 - mixing) * edge[4:8, :] + ratio_rows * edge[0:4, :]) * keep_rows
                return halo + max_step * jnp.tanh(time_step / max_step * speed)

            edge_down.wait_recv()
            edge_up.wait_recv()
            halo_up = moved(halo_up, edge_recv[0])
            halo_down = moved(halo_down, edge_recv[1])
            slots_in.wait_recv()
            points_in = [slot_recv[1, 0:1, :], slot_recv[1, 1:2, :]]

    for i, (source, target) in enumerate([(push_ref, out_push), (decay_ref, out_decay)]):
        stores.append(pltpu.make_async_copy(source, target, out_sem.at[3 + i]))
        stores[-1].start()
    for copy in copies:
        copy.wait_send()
    for store in stores:
        store.wait()


def local(n_tile, n_sec, *arguments):
    displacement, velocity, stiffness, anchor, source, target, weight, _, _ = arguments
    sections, _, rows, columns = displacement.shape
    slots = source.shape[1]
    pieces = columns // 128
    dma = pltpu.SemaphoreType.DMA
    anywhere = pl.BlockSpec(memory_space=pl.ANY)
    scalars = pl.BlockSpec(memory_space=pltpu.SMEM)
    field = jax.ShapeDtypeStruct(displacement.shape, F32)
    gain = jax.ShapeDtypeStruct((sections, columns), F32)
    vmem = pltpu.VMEM
    counts = arguments[7].T
    middle, force, current, push, decay = pl.pallas_call(
        functools.partial(kernel, n_tile, n_sec),
        out_shape=(field, field, field, gain, gain),
        in_specs=[pl.BlockSpec(memory_space=pltpu.HBM)] * 7 + [scalars] * 2,
        out_specs=(anywhere,) * 5,
        scratch_shapes=[
            vmem(displacement.shape, F32),
            vmem(velocity.shape, F32),
            vmem(stiffness.shape, BF16),
            vmem(anchor.shape, F32),
            vmem(source.shape, jnp.int32),
            vmem(target.shape, jnp.int32),
            vmem(weight.shape, F32),
            vmem(stiffness.shape, F32),
            vmem(displacement.shape, F32),
            vmem(displacement.shape, F32),
            vmem((2, 128, 2 * slots), BF16),
            vmem((2, pieces * rows, 2 * slots), F32),
            vmem((sections, columns), F32),
            vmem((sections, columns), F32),
            dma((7,)),
            dma((5,)),
            vmem((16, columns), F32),
            vmem((8, columns), F32),
            vmem((16, columns), F32),
            vmem((8, columns), F32),
            vmem((2, 8, columns), F32),
            vmem((2, 8, columns), F32),
            vmem((2, 8, slots), F32),
            vmem((2, 8, slots), F32),
            vmem((2, 8, slots), F32),
            vmem((2, 8, slots), F32),
            vmem((ITERS, 8, 128), F32),
            vmem((ITERS, n_tile - 1, 8, 128), F32),
            dma((8,)),
            dma((8,)),
            dma((ITERS, n_tile - 1)),
            dma((ITERS, n_tile - 1)),
        ],
        compiler_params=pltpu.CompilerParams(
            collective_id=0, has_side_effects=True, vmem_limit_bytes=60 * 1024 * 1024
        ),
        cost_estimate=pl.CostEstimate(
            flops=40_000_000, bytes_accessed=1_500_000, transcendentals=1_000_000
        ),
    )(*arguments[:7], counts, arguments[8])
    speed = decay[:, None, None, :] * middle + push[:, None, None, :] * force
    return current + max_step * jnp.tanh(time_step * speed / max_step), speed


def solution(mesh):
    placed = (
        P("sec", None, "tile", None),
        P("sec", None, "tile", None),
        P("sec", None, "tile", None),
        P(None, "tile", None),
        P("sec", "tile"),
        P("sec", "tile"),
        P("sec", "tile"),
        P("sec", "tile"),
        P(None, "sec"),
    )
    return jax.shard_map(
        functools.partial(local, mesh.shape["tile"], mesh.shape["sec"]),
        mesh=mesh,
        in_specs=placed,
        out_specs=(P("sec", None, "tile", None), P("sec", None, "tile", None)),
        check_vma=False,
    )
```

```python
import functools

import jax
import jax.numpy as jnp
from jax import lax
from jax.experimental import pallas as pl
from jax.experimental.pallas import tpu as pltpu
from jax.sharding import PartitionSpec as P

ITERS = 2

max_step = 0.05
time_step = 0.5
mixing = 0.1
epsilon = 1e-06
diagonal_rest = 1.4142135623730951
MESH = pl.DeviceIdType.MESH
F32 = jnp.float32
BF16 = jnp.bfloat16


def from_left(values):
    return pltpu.roll(values, 1, 1)


def from_right(values):
    return pltpu.roll(values, values.shape[1] - 1, 1)


def bond(first_gap, second_gap, stiff, rest):
    inverse = lax.rsqrt(first_gap * first_gap + second_gap * second_gap)
    factor = stiff * (1.0 - rest * inverse)
    return factor * first_gap, factor * second_gap


def downward(upper, lower, lower_right, lower_left, stiff):
    south = bond(1.0 + lower[0] - upper[0], lower[1] - upper[1], stiff[0], 1.0)
    east = bond(
        1.0 + lower_right[0] - upper[0], 1.0 + lower_right[1] - upper[1], stiff[1], diagonal_rest
    )
    west = bond(
        1.0 + lower_left[0] - upper[0], lower_left[1] - upper[1] - 1.0, stiff[2], diagonal_rest
    )
    owned = tuple(south[i] + east[i] + west[i] for i in range(2))
    ended = tuple(south[i] + from_left(east[i]) + from_right(west[i]) for i in range(2))
    return owned, ended


def stacked(grid, rows):
    columns = grid.shape[1]
    return jnp.concatenate([grid[:, i : i + 128] for i in range(0, columns, 128)], axis=0)


def unstacked(values, rows):
    return jnp.concatenate([values[i : i + rows] for i in range(0, values.shape[0], rows)], axis=1)


def tables(index, rows, columns):
    pieces = columns // 128
    slots = index.shape[1]
    low = lax.rem(index, 128)
    row = index // columns
    place = (lax.rem(index, columns) // 128) * rows + row
    column_table = (lax.broadcasted_iota(jnp.int32, (128, slots), 0) == low).astype(F32).astype(BF16)
    row_table = (lax.broadcasted_iota(jnp.int32, (pieces * rows, slots), 0) == place).astype(F32)
    return column_table, row_table


def pick(parts, column_table, row_table):
    found = jnp.dot(parts, column_table, preferred_element_type=F32)
    nodes = row_table.shape[0]
    result = []
    for i in range(2):
        both = found[i * nodes : (i + 1) * nodes]
        result.append(jnp.sum(both * row_table, axis=0, keepdims=True))
    return result


def place(amounts, column_table, row_table, rows):
    spread = jnp.concatenate([(x * row_table).astype(BF16) for x in amounts], axis=0)
    out = lax.dot_general(
        spread, column_table, (((1,), (1,)), ((), ())), preferred_element_type=F32
    )
    nodes = row_table.shape[0]
    return [
        unstacked(out[i * nodes : (i + 1) * nodes], rows)
        for i in range(2)
    ]


def kernel(
    n_tile,
    n_sec,
    u_hbm,
    v_hbm,
    k_hbm,
    a_hbm,
    src_hbm,
    tgt_hbm,
    w_hbm,
    cnt,
    rst,
    out_mid,
    out_force,
    out_u,
    out_push,
    out_decay,
    u_ref,
    v_ref,
    k_ref,
    a_ref,
    src_ref,
    tgt_ref,
    w_ref,
    kf_ref,
    force_ref,
    mid_ref,
    ctab_ref,
    rtab_ref,
    push_ref,
    decay_ref,
    in_sem,
    out_sem,
    down_send,
    up_send,
    down_recv,
    up_recv,
    edge_send,
    edge_recv,
    slot_send,
    slot_recv,
    points_send,
    points_recv,
    sums_send,
    sums_recv,
    near_ssem,
    near_rsem,
    sums_ssem,
    sums_rsem,
):
    tile = lax.axis_index("tile")
    sec = lax.axis_index("sec")
    sections, _, rows, columns = u_ref.shape
    slots = src_ref.shape[1]
    below, above = lax.rem(tile + 1, n_tile), lax.rem(tile + n_tile - 1, n_tile)
    after, before = lax.rem(sec + 1, n_sec), lax.rem(sec + n_sec - 1, n_sec)

    loads = [
        pltpu.make_async_copy(source, target, in_sem.at[i])
        for i, (source, target) in enumerate(
            [
                (u_hbm, u_ref),
                (k_hbm, k_ref),
                (src_hbm, src_ref),
                (tgt_hbm, tgt_ref),
                (w_hbm, w_ref),
                (a_hbm, a_ref),
                (v_hbm, v_ref),
            ]
        )
    ]
    for load in loads:
        load.start()

    barrier = pltpu.get_barrier_semaphore()
    for step in range(1, n_tile):
        pl.semaphore_signal(
            barrier, inc=1, device_id=(lax.rem(tile + step, n_tile), sec), device_id_type=MESH
        )
    for other in (after, before):
        pl.semaphore_signal(barrier, inc=1, device_id=(tile, other), device_id_type=MESH)

    def remote(source, target, ssem, rsem, device):
        copy = pltpu.make_async_remote_copy(
            src_ref=source,
            dst_ref=target,
            send_sem=ssem,
            recv_sem=rsem,
            device_id=device,
            device_id_type=MESH,
        )
        copy.start()
        return copy

    def near(number, source, target, device):
        return remote(source, target, near_ssem.at[number], near_rsem.at[number], device)

    for load in loads[:5]:
        load.wait()

    column_ids = lax.broadcasted_iota(jnp.int32, (1, columns), 1)
    has_right = (column_ids < columns - 1).astype(F32)
    has_left = (column_ids >= 1).astype(F32)
    for s in range(sections):
        for i in range(2):
            down_send[2 * s + i : 2 * s + i + 1, :] = u_ref[s, i, rows - 1 : rows, :]
            up_send[2 * s + i : 2 * s + i + 1, :] = u_ref[s, i, 0:1, :]
        for kind in range(4):
            stiff = k_ref[s, kind].astype(F32)
            if kind in (0, 2):
                stiff = stiff * has_right
            if kind == 3:
                stiff = stiff * has_left
            kf_ref[s, kind] = stiff
            if kind > 0:
                at = 8 + 2 * (kind - 1) + s
                down_send[at : at + 1, :] = stiff[rows - 1 : rows, :]

    slot_ids = lax.broadcasted_iota(jnp.int32, (1, slots), 1)
    weights = [
        w_ref[s : s + 1, :] * (slot_ids < cnt[0, s]).astype(F32) for s in range(sections)
    ]

    def store_tables(section, half, index):
        column_table, row_table = tables(index, rows, columns)
        ctab_ref[section, :, half * slots : (half + 1) * slots] = column_table
        rtab_ref[section, :, half * slots : (half + 1) * slots] = row_table

    def picked(section, half, parts):
        lanes = slice(half * slots, (half + 1) * slots)
        return pick(parts, ctab_ref[section, :, lanes], rtab_ref[section, :, lanes])

    def picked_both(section, parts):
        both = pick(parts, ctab_ref[section], rtab_ref[section])
        return [x[:, :slots] for x in both], [x[:, slots:] for x in both]

    def stacked_parts(grids):
        return jnp.concatenate([stacked(grid, rows).astype(BF16) for grid in grids], axis=0)

    def parts_of(section):
        return stacked_parts([u_ref[section, i] for i in range(2)])

    store_tables(1, 0, src_ref[1:2, :])
    store_tables(1, 1, tgt_ref[0:1, :])
    points_1, ends_0 = picked_both(1, parts_of(1))
    slot_send[0, 0:1, :] = tgt_ref[1:2, :].astype(F32)
    slot_send[0, 1:2, :] = weights[1]
    slot_send[0, 2:3, :] = points_1[0]
    slot_send[0, 3:4, :] = points_1[1]

    pl.semaphore_wait(barrier, n_tile + 1)
    copies = [
        near(0, slot_send.at[0], slot_recv.at[0], (tile, after)),
        near(1, down_send, down_recv, (below, sec)),
        near(2, up_send, up_recv, (above, sec)),
    ]
    slots_in, down_in, up_in = copies

    store_tables(0, 0, src_ref[0:1, :])
    points_0 = picked(0, 0, parts_of(0))
    loads[5].wait()
    first_sec = sec == 0

    def slab_parts():
        return stacked_parts([jnp.where(first_sec, a_ref[i], u_ref[0, i]) for i in range(2)])

    slots_in.wait_recv()
    store_tables(0, 1, slot_recv[0, 0:1, :].astype(jnp.int32))
    weight_in = slot_recv[0, 1:2, :] * jnp.where(first_sec, 0.0, 1.0)
    ends_in = picked(0, 1, slab_parts())
    points_in = [slot_recv[0, 2:3, :], slot_recv[0, 3:4, :]]
    points_send[0, 0:1, :] = ends_in[0]
    points_send[0, 1:2, :] = ends_in[1]
    points = near(3, points_send.at[0], points_recv.at[0], (tile, before))
    copies.append(points)

    loads[6].wait()
    not_last = jnp.where(tile == n_tile - 1, 0.0, 1.0)
    not_first = jnp.where(tile == 0, 0.0, 1.0)
    row_ids = lax.broadcasted_iota(jnp.int32, (rows, columns), 0)
    row_valid = jnp.where(row_ids == rows - 1, not_last, 1.0)
    for s in range(sections):
        for kind in range(1, 4):
            kf_ref[s, kind] = kf_ref[s, kind] * row_valid

    down_in.wait_recv()
    up_in.wait_recv()
    halo_up = down_recv[0:4, :]
    halo_down = up_recv[0:4, :]
    stiff_up = [down_recv[8 + 2 * i : 10 + 2 * i, :] * not_first for i in range(3)]
    speed_ratio = None

    for iteration in range(ITERS):
        upper = [
            jnp.concatenate([halo_up[i : i + 1], halo_up[2 + i : 3 + i]], axis=0)
            for i in range(2)
        ]
        lower = [
            jnp.concatenate([u_ref[0, i, 0:1, :], u_ref[1, i, 0:1, :]], axis=0)
            for i in range(2)
        ]
        _, ended_up = downward(
            upper,
            lower,
            [from_right(x) for x in lower],
            [from_left(x) for x in lower],
            stiff_up,
        )
        for s in range(sections):
            own = [u_ref[s, i] for i in range(2)]
            right = [from_right(x) for x in own]
            left = [from_left(x) for x in own]
            tail = [halo_down[2 * s + i : 2 * s + i + 1] for i in range(2)]
            lower = [jnp.concatenate([own[i][1:], tail[i]], axis=0) for i in range(2)]
            lower_right = [
                jnp.concatenate([right[i][1:], from_right(tail[i])], axis=0) for i in range(2)
            ]
            lower_left = [
                jnp.concatenate([left[i][1:], from_left(tail[i])], axis=0) for i in range(2)
            ]
            owned, ended = downward(
                own, lower, lower_right, lower_left, [kf_ref[s, kind] for kind in (1, 2, 3)]
            )
            east = bond(right[0] - own[0], 1.0 + right[1] - own[1], kf_ref[s, 0], 1.0)
            for i in range(2):
                incoming = jnp.concatenate(
                    [ended_up[i][s : s + 1], ended[i][: rows - 1]], axis=0
                )
                force_ref[s, i] = owned[i] + east[i] - from_left(east[i]) - incoming

        match_0 = [weights[0] * (ends_0[i] - points_0[i]) for i in range(2)]
        match_in = [weight_in * (ends_in[i] - points_in[i]) for i in range(2)]
        added = place(
            [jnp.concatenate([match_0[i], -match_in[i]], axis=1) for i in range(2)],
            ctab_ref[0],
            rtab_ref[0],
            rows,
        )
        for i in range(2):
            force_ref[0, i] = force_ref[0, i] + added[i]
        points.wait_recv()
        match_1 = [
            weights[1] * (points_recv[iteration, i : i + 1, :] - points_1[i]) for i in range(2)
        ]
        added = place(
            [jnp.concatenate([match_1[i], -match_0[i]], axis=1) for i in range(2)],
            ctab_ref[1],
            rtab_ref[1],
            rows,
        )
        for i in range(2):
            force_ref[1, i] = force_ref[1, i] + added[i]

        for s in range(sections):
            force_sq, speed_sq = 0.0, 0.0
            for i in range(2):
                force = force_ref[s, i]
                middle = v_ref[s, i] + time_step * force
                mid_ref[s, i] = middle
                force_sq = force_sq + jnp.sum(force * force, axis=0, keepdims=True)
                speed_sq = speed_sq + jnp.sum(middle * middle, axis=0, keepdims=True)
                if iteration < ITERS - 1:
                    at = 2 * s + i
                    edge_send[0, at : at + 1, :] = force[rows - 1 : rows, :]
                    edge_send[0, 4 + at : 5 + at, :] = middle[rows - 1 : rows, :]
                    edge_send[1, at : at + 1, :] = force[0:1, :]
                    edge_send[1, 4 + at : 5 + at, :] = middle[0:1, :]
            for at, value in ((s, force_sq), (2 + s, speed_sq)):
                narrow = value[:, 0:128]
                for piece in range(128, columns, 128):
                    narrow = narrow + value[:, piece : piece + 128]
                sums_send[iteration, at : at + 1, :] = narrow
        peers = []
        for step in range(n_tile - 1, 0, -1):
            peers.append(
                remote(
                    sums_send.at[iteration],
                    sums_recv.at[iteration, step - 1],
                    sums_ssem.at[iteration, step - 1],
                    sums_rsem.at[iteration, step - 1],
                    (lax.rem(tile + step, n_tile), sec),
                )
            )
        copies += peers
        if iteration < ITERS - 1:
            edge_down = near(4, edge_send.at[0], edge_recv.at[0], (below, sec))
            edge_up = near(5, edge_send.at[1], edge_recv.at[1], (above, sec))
            copies += [edge_down, edge_up]

        if iteration == ITERS - 1:
            stores = [
                pltpu.make_async_copy(source, target, out_sem.at[i])
                for i, (source, target) in enumerate(
                    [(mid_ref, out_mid), (force_ref, out_force), (u_ref, out_u)]
                )
            ]
            for store in stores:
                store.start()

        total = sums_send[iteration, 0:4, :]
        for peer in peers:
            peer.wait_recv()
        for step in range(n_tile - 1):
            total = total + sums_recv[iteration, step, 0:4, :]
        total = jnp.sum(total, axis=1, keepdims=True)
        ratio = jnp.sqrt(total[2:4]) / jnp.sqrt(total[0:2] + epsilon)
        keep = [(1 - rst[iteration, s]).astype(F32) for s in range(sections)]

        if iteration == ITERS - 1:
            for s in range(sections):
                push_ref[s : s + 1, :] = jnp.broadcast_to(
                    mixing * ratio[s : s + 1, :] * keep[s], (1, columns)
                )
                decay_ref[s : s + 1, :] = jnp.full((1, columns), (1.0 - mixing) * keep[s], F32)
            break

        for s in range(sections):
            push = mixing * ratio[s : s + 1, :]
            for i in range(2):
                speed = ((1.0 - mixing) * mid_ref[s, i] + push * force_ref[s, i]) * keep[s]
                v_ref[s, i] = speed
                u_ref[s, i] = u_ref[s, i] + max_step * jnp.tanh(time_step / max_step * speed)

        if iteration < ITERS - 1:
            points_1, ends_0 = picked_both(1, parts_of(1))
            slot_send[1, 0:1, :] = points_1[0]
            slot_send[1, 1:2, :] = points_1[1]
            slots_in = near(6, slot_send.at[1], slot_recv.at[1], (tile, after))
            ends_in = picked(0, 1, slab_parts())
            points_send[1, 0:1, :] = ends_in[0]
            points_send[1, 1:2, :] = ends_in[1]
            points = near(7, points_send.at[1], points_recv.at[1], (tile, before))
            copies += [slots_in, points]
            points_0 = picked(0, 0, parts_of(0))

            half = lax.broadcasted_iota(jnp.int32, (4, columns), 0) < 2
            ratio_rows = jnp.where(half, mixing * ratio[0:1, :], mixing * ratio[1:2, :])
            keep_rows = jnp.where(half, keep[0], keep[1])

            def moved(halo, edge):
                speed = ((1.0 - mixing) * edge[4:8, :] + ratio_rows * edge[0:4, :]) * keep_rows
                return halo + max_step * jnp.tanh(time_step / max_step * speed)

            edge_down.wait_recv()
            edge_up.wait_recv()
            halo_up = moved(halo_up, edge_recv[0])
            halo_down = moved(halo_down, edge_recv[1])
            slots_in.wait_recv()
            points_in = [slot_recv[1, 0:1, :], slot_recv[1, 1:2, :]]

    for i, (source, target) in enumerate([(push_ref, out_push), (decay_ref, out_decay)]):
        stores.append(pltpu.make_async_copy(source, target, out_sem.at[3 + i]))
        stores[-1].start()
    for copy in copies:
        copy.wait_send()
    for store in stores:
        store.wait()


def local(n_tile, n_sec, *arguments):
    displacement, velocity, stiffness, anchor, source, target, weight, _, _ = arguments
    sections, _, rows, columns = displacement.shape
    slots = source.shape[1]
    pieces = columns // 128
    dma = pltpu.SemaphoreType.DMA
    anywhere = pl.BlockSpec(memory_space=pl.ANY)
    scalars = pl.BlockSpec(memory_space=pltpu.SMEM)
    field = jax.ShapeDtypeStruct(displacement.shape, F32)
    gain = jax.ShapeDtypeStruct((sections, columns), F32)
    vmem = pltpu.VMEM
    counts = arguments[7].T
    middle, force, current, push, decay = pl.pallas_call(
        functools.partial(kernel, n_tile, n_sec),
        out_shape=(field, field, field, gain, gain),
        in_specs=[pl.BlockSpec(memory_space=pltpu.HBM)] * 7 + [scalars] * 2,
        out_specs=(anywhere,) * 5,
        scratch_shapes=[
            vmem(displacement.shape, F32),
            vmem(velocity.shape, F32),
            vmem(stiffness.shape, BF16),
            vmem(anchor.shape, F32),
            vmem(source.shape, jnp.int32),
            vmem(target.shape, jnp.int32),
            vmem(weight.shape, F32),
            vmem(stiffness.shape, F32),
            vmem(displacement.shape, F32),
            vmem(displacement.shape, F32),
            vmem((2, 128, 2 * slots), BF16),
            vmem((2, pieces * rows, 2 * slots), F32),
            vmem((sections, columns), F32),
            vmem((sections, columns), F32),
            dma((7,)),
            dma((5,)),
            vmem((16, columns), F32),
            vmem((8, columns), F32),
            vmem((16, columns), F32),
            vmem((8, columns), F32),
            vmem((2, 8, columns), F32),
            vmem((2, 8, columns), F32),
            vmem((2, 8, slots), F32),
            vmem((2, 8, slots), F32),
            vmem((2, 8, slots), F32),
            vmem((2, 8, slots), F32),
            vmem((ITERS, 8, 128), F32),
            vmem((ITERS, n_tile - 1, 8, 128), F32),
            dma((8,)),
            dma((8,)),
            dma((ITERS, n_tile - 1)),
            dma((ITERS, n_tile - 1)),
        ],
        compiler_params=pltpu.CompilerParams(
            collective_id=0, has_side_effects=True, vmem_limit_bytes=60 * 1024 * 1024
        ),
        cost_estimate=pl.CostEstimate(
            flops=40_000_000, bytes_accessed=1_500_000, transcendentals=1_000_000
        ),
    )(*arguments[:7], counts, arguments[8])
    speed = decay[:, None, None, :] * middle + push[:, None, None, :] * force
    return current + max_step * jnp.tanh(time_step * speed / max_step), speed


def solution(mesh):
    placed = (
        P("sec", None, "tile", None),
        P("sec", None, "tile", None),
        P("sec", None, "tile", None),
        P(None, "tile", None),
        P("sec", "tile"),
        P("sec", "tile"),
        P("sec", "tile"),
        P("sec", "tile"),
        P(None, "sec"),
    )
    return jax.shard_map(
        functools.partial(local, mesh.shape["tile"], mesh.shape["sec"]),
        mesh=mesh,
        in_specs=placed,
        out_specs=(P("sec", None, "tile", None), P("sec", None, "tile", None)),
        check_vma=False,
    )
```
